32 devices in a mesh: groups: 2 (over x), expert: 16 (over z, y, core), dp: 1.
Axes of the slice: x: 2, y: 2, z: 4, core: 2. Of those that a mesh axis runs over, the one named last changes fastest.
Arguments:
- queries: bfloat16 [4, 64, 64, 576], P(None, ('groups', 'expert', 'dp')), parts along dimension 1, may hold values from -400 to 400
- latent_cache: bfloat16 [64, 256, 576], P(('groups', 'expert', 'dp')), parts along dimension 0, may hold values from -8 to 8
- new_latents: bfloat16 [4, 64, 576], P(None, ('groups', 'expert', 'dp')), parts along dimension 1, may hold values from -8 to 8
- lengths: int32 [64], P(('groups', 'expert', 'dp')), parts along dimension 0, may hold values from 2 to 252, as said below
- hidden_in: bfloat16 [4, 64, 3584], P(None, ('groups', 'expert', 'dp')), parts along dimension 1, may hold values from -6 to 6
- first_routes: int32 [2, 64, 8], P(None, ('groups', 'expert')), parts along dimension 1, may hold values from 0 to 15, all different within a row; in each aligned block of 4 rows (0 to 3, 4 to 7, ..., all dimensions but the last counted through in order) at most 4 rows name the same one
- second_routes: int32 [2, 64, 8], P(None, ('groups', 'expert')), parts along dimension 1, may hold values from 0 to 17, all different within a row; in each aligned block of 4 rows (0 to 3, 4 to 7, ..., all dimensions but the last counted through in order) at most 4 rows name the same one
- route_weights: float32 [4, 64, 8], P(None, ('groups', 'expert')), parts along dimension 1, may hold values from 0.05 to 1
- gate_weights: bfloat16 [16, 3584, 1024], P('expert', None, 'dp'), may hold values from -0.09375 to 0.09375
- up_weights: bfloat16 [16, 3584, 1024], P('expert', None, 'dp'), may hold values from -0.09375 to 0.09375
- down_weights: bfloat16 [16, 1024, 3584], P('expert', 'dp'), may hold values from -0.1875 to 0.1875
- hot_experts: int32 [2], replicated, may hold values from 0 to 15
Outputs:
- context: bfloat16 [4, 64, 64, 512], P(None, ('groups', 'expert', 'dp')), parts along dimension 1
- moe_out: bfloat16 [4, 64, 3584], P(None, ('groups', 'expert', 'dp')), parts along dimension 1
The draws below stay inside these ranges and needn't reach their ends.
There are 2 independent parts, one for each index of `groups`. The reference program is written for one: setup_inputs(seed, part) draws one part's arguments, and reference() takes and returns one part's arrays. A program takes and returns all parts, laid end to end along the dimension named above; an argument that names none is the same for every part. Nothing has to cross between parts.
Inputs may be any that keep to these rules, and one draw needn't show every extreme that they name: `lengths`: each row holds at least 2 filled slots; some row of every draw holds exactly 252. `first_routes`: each row names 8 distinct experts. In every step the 4 rows held by one index of expert name no expert more than 4 times, and in some steps and indices one expert exactly 4 times. `second_routes`: each row names 8 distinct slots; slot 16 + r stands for the copy of hot_experts[r]. In every step the 4 rows held by one index of expert name no slot more than 4 times, and in some steps and indices one slot exactly 4 times.
All inputs are finite; a program needn't handle non-finite values.
Results may differ from the reference program's by a relative error of at most 0.015.
Values may be sent and summed in bfloat16 or wider, within the bound.
No kernel may reach another device: no remote copies, remote signals or barrier semaphores. Data moves between devices by JAX's collectives and lax.ppermute only.
A program may use at most 192 MiB of HBM per device.

```python
import math
import jax
import jax.numpy as jnp
import numpy as np
from jax import lax

D = 3584
EXPERT_FF = 1024
HEADS = 64
RANK = 512
TOP = 8
REPL = 2
PRE = 2
POST = 2
B_DEV = 2
CACHE = 256
LAT = 576
STEPS = 4
EXPERTS = 16
BATCH = 32
CAP = 4


def cache_base(key):
    values = jax.random.normal(key, (BATCH, CACHE, LAT), jnp.float32)
    return jnp.clip(values, -6.0, 6.0)


def draw_latent_cache(key, part):
    base_values = cache_base(key)
    return base_values.astype(jnp.bfloat16)


def draw_queries(key, part):
    key = jax.random.fold_in(key, 5)
    values = jnp.clip(jax.random.normal(key, (STEPS, BATCH, HEADS, LAT), jnp.float32), -6.0, 6.0)
    values = jnp.clip(values, -400.0, 400.0)
    return values.astype(jnp.bfloat16)


def draw_lengths(key, part):
    key = jax.random.fold_in(key, 7)
    longest = CACHE - STEPS
    values = jax.random.randint(key, (BATCH,), 2, longest + 1, jnp.int32)
    chosen = jax.random.randint(jax.random.fold_in(key, 1), (), 0, BATCH, jnp.int32)
    return jnp.where(jnp.arange(BATCH, dtype=jnp.int32) == chosen, longest, values).astype(jnp.int32)


def block_scale(rng, extent, pieces, least, high):
    gain = 1.0
    for dim, shards_of in pieces:
        steps = jax.random.uniform(jax.random.fold_in(jax.random.fold_in(rng, 6), dim), (shards_of,), jnp.float32, least / len(pieces), high / len(pieces))
        gain = gain * jnp.repeat(jnp.exp(steps), extent[dim] // shards_of).reshape((-1,) + (1,) * (len(extent) - 1 - dim))
    return gain


def assign_block(rng, own, number, rows, count, top, bound, lean):
    order = jax.random.permutation(rng, count)
    crowded, ordinary = portions_of(count, rows * top, bound, lean, True), portions_of(count, rows * top, bound, lean, False)
    places = jnp.arange(count)

    def named(sizes, offset_by):
        used = int((sizes > 0).sum())
        fixed = max(1, used // 4)
        moved = fixed + (places - fixed + offset_by * (used - fixed)) % max(1, count - fixed)
        return jnp.zeros((count,), jnp.int32).at[order[jnp.where(places < fixed, places, moved)]].set(jnp.asarray(sizes, jnp.int32))

    sizes = jnp.where(number % 4 == 0, named(crowded, number // 4), named(ordinary, number - number // 4 - 1))
    mixed = jax.random.permutation(jax.random.fold_in(own, 3), count)
    source_of, receiver = mixed[0:count // 2 * 2:2], mixed[1:count // 2 * 2:2]
    room = jnp.minimum(sizes[source_of] - 1, bound - sizes[receiver]) // 2
    room = jnp.where((source_of == order[0]) | (receiver == order[0]) | (sizes[receiver] == 0), 0, jnp.maximum(room, 0))
    moved = jax.random.randint(jax.random.fold_in(own, 4), (count // 2,), 0, 1 << 20) % (room + 1)
    sizes = sizes.at[source_of].add(-moved).at[receiver].add(moved)
    items = jnp.searchsorted(jnp.cumsum(sizes), jnp.arange(rows * top), side="right").astype(jnp.int32)
    listing = items.reshape(top, rows).T
    listing = listing[jax.random.permutation(jax.random.fold_in(own, 1), rows)]
    offset_by = jax.random.randint(jax.random.fold_in(own, 2), (rows, 1), 0, top)
    return jnp.take_along_axis(listing, (jnp.arange(top)[None, :] + offset_by) % top, axis=1)


def portions_of(amount, total, most, lean, full):
    weights = [(1 << 20) // math.isqrt(standing ** lean) + 1 for standing in range(1, amount + 1)]
    largest = most if full else min(most, max(-(-total // amount), total * weights[0] // sum(weights)))
    least = 1 if total - largest >= amount - 1 else 0
    given, spare = [largest] + [least] * (amount - 1), total - largest - least * (amount - 1)
    while spare > 0:
        free = [i for i in range(1, amount) if given[i] < largest] or [i for i in range(1, amount) if given[i] < most]
        whole, budget = sum([weights[i] for i in free]), spare
        for i in free:
            addition = min(most - given[i], max(1, budget * weights[i] // whole), spare)
            given[i] = given[i] + addition
            spare = spare - addition
    return np.array(given)


def scatter_about(stream_key, shape, scale, most, split=(), kind=jnp.bfloat16):
    result = jax.random.normal(stream_key, shape, jnp.float32) * scale
    if len(split) > 0:
        result = block_scale(stream_key, shape, split, -0.22, 0.18) * result
    return jnp.clip(result, min=-most, max=most).astype(kind)


def setup_inputs(seed: int = 0, part: int = 0) -> dict:
    key_of = jax.random.split(jax.random.key(seed), 13)
    part_splits = jax.random.split(jax.random.fold_in(key_of[12], part), 13)
    queries = draw_queries(jax.random.fold_in(jax.random.fold_in(key_of[12], part), 71), part)
    latent_cache = draw_latent_cache(jax.random.fold_in(jax.random.fold_in(key_of[12], part), 71), part)
    new_latents = scatter_about(part_splits[2], (STEPS, BATCH, LAT), 1.5, 8.0, ((1, 16),))
    lengths = draw_lengths(jax.random.fold_in(jax.random.fold_in(key_of[12], part), 71), part)
    hidden_in = scatter_about(part_splits[4], (STEPS, BATCH, D), 1.0, 6.0, ((1, 16),))
    first_routes_keys = jax.random.split(jax.random.fold_in(part_splits[5], 1), PRE * BATCH // (2 * B_DEV))
    first_routes_turns = jax.random.permutation(jax.random.fold_in(part_splits[5], 3), PRE * BATCH // (2 * B_DEV))
    first_routes = jax.vmap(lambda own, number: assign_block(jax.random.fold_in(part_splits[5], 2), own, number, 2 * B_DEV, EXPERTS, TOP, CAP, 2))(first_routes_keys, first_routes_turns).reshape((PRE, BATCH, TOP))
    second_routes_keys = jax.random.split(jax.random.fold_in(part_splits[6], 1), POST * BATCH // (2 * B_DEV))
    second_routes_turns = jax.random.permutation(jax.random.fold_in(part_splits[6], 3), POST * BATCH // (2 * B_DEV))
    second_routes = jax.vmap(lambda own, number: assign_block(jax.random.fold_in(part_splits[6], 2), own, number, 2 * B_DEV, EXPERTS + REPL, TOP, CAP, 0))(second_routes_keys, second_routes_turns).reshape((POST, BATCH, TOP))
    route_weights = jnp.clip(jnp.exp(math.log(1.0) - 2.9957323 * jax.random.uniform(part_splits[7], (STEPS, BATCH, TOP), jnp.float32) ** block_scale(part_splits[7], (STEPS, BATCH, TOP), ((1, 16),), -0.2, 0.2)), 0.05, 1.0)
    gate_weights = scatter_about(key_of[8], (EXPERTS, D, EXPERT_FF), D ** -0.5, 0.09375, ((0, 16),))
    up_weights = scatter_about(key_of[9], (EXPERTS, D, EXPERT_FF), D ** -0.5, 0.09375, ((0, 16),))
    down_weights = scatter_about(key_of[10], (EXPERTS, EXPERT_FF, D), EXPERT_FF ** -0.5, 0.1875, ((0, 16),))
    hot_experts = jax.random.randint(key_of[11], (REPL,), 0, EXPERTS).astype(jnp.int32)
    return {"queries": queries, "latent_cache": latent_cache, "new_latents": new_latents, "lengths": lengths, "hidden_in": hidden_in, "first_routes": first_routes, "second_routes": second_routes, "route_weights": route_weights, "gate_weights": gate_weights, "up_weights": up_weights, "down_weights": down_weights, "hot_experts": hot_experts}


SCORE_SCALE = 0.07216878364870322


def expert_apply(token_rows, gate_weight, up_weight, down_weight):
    gate_act = jnp.dot(token_rows, gate_weight, preferred_element_type=jnp.float32)
    up_act = jnp.dot(token_rows, up_weight, preferred_element_type=jnp.float32)
    hidden_act = (jax.nn.silu(gate_act) * up_act).astype(jnp.bfloat16)
    return jnp.dot(hidden_act, down_weight, preferred_element_type=jnp.float32)


def attend(queries_now, latent_cache, new_latents, lengths, step_index):
    query_f = queries_now.astype(jnp.float32)
    cache_f = latent_cache.astype(jnp.float32)
    fresh_f = new_latents.astype(jnp.float32)
    old_scores = jnp.einsum('bhl,bjl->bhj', query_f, cache_f) * SCORE_SCALE
    new_scores = jnp.einsum('bhl,tbl->bht', query_f, fresh_f) * SCORE_SCALE
    keep_old = (jnp.arange(latent_cache.shape[1], dtype=jnp.int32)[None, :] < lengths[:, None])[:, None, :]
    keep_new = (jnp.arange(new_latents.shape[0], dtype=jnp.int32) <= step_index)[None, None, :]
    old_scores = jnp.where(keep_old, old_scores, -1e30)
    new_scores = jnp.where(keep_new, new_scores, -1e30)
    row_max = jnp.maximum(jnp.max(old_scores, axis=2, keepdims=True), jnp.max(new_scores, axis=2, keepdims=True))
    old_exp = jnp.where(keep_old, jnp.exp(old_scores - row_max), 0.0)
    new_exp = jnp.where(keep_new, jnp.exp(new_scores - row_max), 0.0)
    denominator = jnp.sum(old_exp, axis=2, keepdims=True) + jnp.sum(new_exp, axis=2, keepdims=True)
    old_probs = lax.optimization_barrier((old_exp / denominator).astype(jnp.bfloat16))
    new_probs = lax.optimization_barrier((new_exp / denominator).astype(jnp.bfloat16))
    context = jnp.einsum('bhj,bjr->bhr', old_probs.astype(jnp.float32), cache_f[:, :, :RANK])
    context = context + jnp.einsum('bht,tbr->bhr', new_probs.astype(jnp.float32), fresh_f[:, :, :RANK])
    return context.astype(jnp.bfloat16)


def mixture(token_rows, chosen, weights, gate_weights, up_weights, down_weights):
    experts_all = jnp.arange(EXPERTS, dtype=jnp.int32)
    coefficient = jnp.sum(weights[:, :, None] * (chosen[:, :, None] == experts_all[None, None, :]).astype(jnp.float32), axis=1)

    def add_expert(summed, item):
        gate_weight, up_weight, down_weight, column = item
        return summed + column[:, None] * expert_apply(token_rows, gate_weight, up_weight, down_weight), None

    zeros = jnp.zeros((token_rows.shape[0], token_rows.shape[1]), jnp.float32)
    summed, _ = lax.scan(add_expert, zeros, (gate_weights, up_weights, down_weights, jnp.transpose(coefficient)))
    return summed.astype(jnp.bfloat16)


def reference(queries, latent_cache, new_latents, lengths, hidden_in, first_routes, second_routes, route_weights, gate_weights, up_weights, down_weights, hot_experts):
    contexts = []
    outputs = []
    for step_index in range(STEPS):
        contexts.append(attend(queries[step_index], latent_cache, new_latents, lengths, step_index))
        if step_index < PRE:
            chosen = first_routes[step_index]
        else:
            slots = second_routes[step_index - PRE]
            replica_index = jnp.clip(slots - EXPERTS, 0, REPL - 1).astype(jnp.int32)
            chosen = jnp.where(slots < EXPERTS, slots, hot_experts[replica_index]).astype(jnp.int32)
        outputs.append(mixture(hidden_in[step_index], chosen, route_weights[step_index], gate_weights, up_weights, down_weights))
    return jnp.stack(contexts, axis=0), jnp.stack(outputs, axis=0)
```

```python
import functools

import jax
import jax.numpy as jnp
from jax import lax
from jax.experimental import pallas as pl
from jax.experimental.pallas import tpu as pltpu
from jax.sharding import PartitionSpec as P

RANK = 512
SCORE_SCALE = 0.07216878364870322
LANES = 128
PEERS = ("expert", "dp")
MIB = 1 << 20

VMEM = pl.BlockSpec(memory_space=pltpu.VMEM)
SMEM = pl.BlockSpec(memory_space=pltpu.SMEM)
ANY = pl.BlockSpec(memory_space=pl.ANY)


def pack_kernel(experts, hidden_ref, first_ref, second_ref, weights_ref, hot_ref, out_ref):
    steps, rows_dev, width = hidden_ref.shape
    before, _, top = first_ref.shape
    tail = out_ref.shape[1] - width
    column = lax.broadcasted_iota(jnp.int32, (rows_dev, tail), 1)
    rows, marks = [], []
    for step in range(steps):
        if step < before:
            chosen = first_ref[step]
        else:
            chosen = second_ref[step - before]
            for replica in range(hot_ref.shape[0]):
                chosen = jnp.where(chosen == experts + replica, hot_ref[replica], chosen)
        weight = weights_ref[step]
        total = jnp.zeros((rows_dev, tail), jnp.float32)
        for k in range(top):
            picked = chosen[:, k : k + 1]
            here = (column == picked) | (column == picked + experts)
            total = total + jnp.where(here, weight[:, k : k + 1], 0.0)
        high = total.astype(jnp.bfloat16).astype(jnp.float32)
        rows.append(hidden_ref[step].astype(jnp.float32))
        marks.append(jnp.where(column < experts, high, total - high))
    out_ref[:, :width] = jnp.concatenate(rows, axis=0).astype(jnp.bfloat16)
    out_ref[:, width:] = jnp.concatenate(marks, axis=0).astype(jnp.bfloat16)


def attend_kernel(queries_ref, cache_ref, new_ref, lengths_ref, out_ref, keys):
    steps, rows_dev, heads, _ = queries_ref.shape
    slots = cache_ref.shape[1]
    tail = 16
    fresh = [new_ref[t].astype(jnp.float32) for t in range(steps)]
    for b in range(rows_dev):
        keys[0 : slots - tail] = cache_ref[b, 0 : slots - tail]
        last = cache_ref[b, slots - tail : slots].astype(jnp.float32)
        last = jnp.concatenate([last[: tail - steps]] + [f[b : b + 1] for f in fresh], axis=0)
        keys[slots - tail : slots] = last.astype(jnp.bfloat16)
        queries = queries_ref[:, b].reshape(steps * heads, queries_ref.shape[3])
        scores = lax.dot_general(
            queries, keys[...], (((1,), (1,)), ((), ())), preferred_element_type=jnp.float32
        )
        scores = scores * SCORE_SCALE
        place = lax.broadcasted_iota(jnp.int32, scores.shape, 1)
        step = lax.broadcasted_iota(jnp.int32, scores.shape, 0) // heads
        age = place - (slots - steps)
        keep = (place < lengths_ref[b]) | ((age >= 0) & (age <= step))
        scores = jnp.where(keep, scores, -1e30)
        weight = jnp.exp(scores - jnp.max(scores, axis=1, keepdims=True))
        probs = weight / jnp.sum(weight, axis=1, keepdims=True)
        context = jnp.dot(
            probs.astype(jnp.bfloat16), keys[:, :RANK], preferred_element_type=jnp.float32
        )
        out_ref[:, b] = context.astype(jnp.bfloat16).reshape(steps, heads, RANK)


def expert_kernel(experts, tile, *refs):
    x_refs = refs[:4]
    own_ref, gate_hbm, up_hbm, down_hbm, keep_ref, send_ref = refs[4:10]
    x, gate, up, down, hidden, sems = refs[10:]
    width = down_hbm.shape[2]
    units = down_hbm.shape[1]
    parts = units // tile
    columns = width // parts
    copies = []
    for j in range(parts):
        cut = pl.ds(j * tile, tile)
        copies.append(pltpu.make_async_copy(gate_hbm.at[0, :, cut], gate.at[:, cut], sems.at[0, j]))
        copies.append(pltpu.make_async_copy(up_hbm.at[0, :, cut], up.at[:, cut], sems.at[1, j]))
    for j in range(parts):
        cut = pl.ds(j * columns, columns)
        copies.append(
            pltpu.make_async_copy(down_hbm.at[0, :, cut], down.at[:, cut], sems.at[2, j])
        )
    for copy in copies:
        copy.start()
    piece = x_refs[0].shape[0]
    for i, x_ref in enumerate(x_refs):
        x[i * piece : (i + 1) * piece] = x_ref[...]
    own = own_ref[0]
    marks = x[:, width:].astype(jnp.float32)
    column = lax.broadcasted_iota(jnp.int32, marks.shape, 1)
    here = (column == own) | (column == own + experts)
    share = jnp.sum(jnp.where(here, marks, 0.0), axis=1, keepdims=True)
    for j in range(parts):
        cut = slice(j * tile, (j + 1) * tile)
        copies[2 * j].wait()
        gate_act = jnp.dot(x[:, :width], gate[:, cut], preferred_element_type=jnp.float32)
        copies[2 * j + 1].wait()
        up_act = jnp.dot(x[:, :width], up[:, cut], preferred_element_type=jnp.float32)
        act = gate_act / (1.0 + jnp.exp(-gate_act)) * up_act
        hidden[:, cut] = act.astype(jnp.bfloat16)
    half = 2 * piece
    for j in range(parts):
        cut = slice(j * columns, (j + 1) * columns)
        copies[2 * parts + j].wait()
        out = jnp.dot(hidden[...], down[:, cut], preferred_element_type=jnp.float32) * share
        keep_ref[:, cut] = out[:half].astype(jnp.bfloat16)
        send_ref[:, cut] = out[half:].astype(jnp.bfloat16)


def sum_kernel(*refs):
    *in_refs, out_ref = refs
    steps, rows_dev, _ = out_ref.shape
    total = in_refs[0][...].astype(jnp.float32)
    for ref in in_refs[1:]:
        total = total + ref[...].astype(jnp.float32)
    total = total.astype(jnp.bfloat16).astype(jnp.float32)
    for step in range(steps):
        out_ref[step] = total[step * rows_dev : (step + 1) * rows_dev].astype(jnp.bfloat16)


def swap(value, mask):
    size = lax.axis_size(PEERS)
    return lax.ppermute(value, PEERS, [(i, i ^ mask) for i in range(size)])


def per_device(
    queries,
    latent_cache,
    new_latents,
    lengths,
    hidden_in,
    first_routes,
    second_routes,
    route_weights,
    gate_weights,
    up_weights,
    down_weights,
    hot_experts,
):
    experts = lax.axis_size("expert")
    devices = lax.axis_size(PEERS)
    steps, rows_dev, width = hidden_in.shape
    rows = steps * rows_dev
    units = down_weights.shape[1]
    bits = devices.bit_length() - 1
    if first_routes.shape[1] != rows_dev:
        begin = lax.axis_index("dp") * rows_dev
        first_routes = lax.dynamic_slice_in_dim(first_routes, begin, rows_dev, 1)
        second_routes = lax.dynamic_slice_in_dim(second_routes, begin, rows_dev, 1)
        route_weights = lax.dynamic_slice_in_dim(route_weights, begin, rows_dev, 1)

    tail = -(-2 * experts // LANES) * LANES
    packed = pl.pallas_call(
        functools.partial(pack_kernel, experts),
        out_shape=jax.ShapeDtypeStruct((rows, width + tail), jnp.bfloat16),
        in_specs=[VMEM, VMEM, VMEM, VMEM, SMEM],
        out_specs=VMEM,
        compiler_params=pltpu.CompilerParams(vmem_limit_bytes=4 * MIB),
        name="pack",
    )(hidden_in, first_routes, second_routes, route_weights, hot_experts)

    high = devices // 4
    blocks = [packed] + [swap(packed, k * high) for k in range(1, 4)]
    held = jnp.concatenate(blocks, axis=0)
    for bit in range(bits - 3, 1, -1):
        held = jnp.concatenate([held, swap(held, 1 << bit)], axis=0)
    second = swap(held, 2)
    other = swap(held, 1)
    other_second = swap(second, 1)

    count = 4 * held.shape[0]
    half = count // 2
    tile = min(256, units)
    parts = units // tile
    own = lax.axis_index("expert").astype(jnp.int32).reshape(1)
    keep, send = pl.pallas_call(
        functools.partial(expert_kernel, experts, tile),
        out_shape=[jax.ShapeDtypeStruct((half, width), jnp.bfloat16)] * 2,
        in_specs=[VMEM] * 4 + [SMEM] + [ANY] * 3,
        out_specs=[VMEM, VMEM],
        scratch_shapes=[
            pltpu.VMEM((count, width + tail), jnp.bfloat16),
            pltpu.VMEM((width, units), jnp.bfloat16),
            pltpu.VMEM((width, units), jnp.bfloat16),
            pltpu.VMEM((units, width), jnp.bfloat16),
            pltpu.VMEM((count, units), jnp.bfloat16),
            pltpu.SemaphoreType.DMA((3, parts)),
        ],
        compiler_params=pltpu.CompilerParams(vmem_limit_bytes=48 * MIB),
        cost_estimate=pl.CostEstimate(
            flops=6 * count * width * units,
            bytes_accessed=6 * width * units,
            transcendentals=count * units,
        ),
        name="experts",
    )(held, second, other, other_second, own, gate_weights, up_weights, down_weights)

    back = swap(send, 1)
    value = keep.astype(jnp.float32) + back.astype(jnp.float32)
    for bit in range(1, bits - 2):
        size = value.shape[0] // 2
        back = swap(value[size:].astype(jnp.bfloat16), 1 << bit)
        value = value[:size] + back.astype(jnp.float32)
    value = value.astype(jnp.bfloat16)
    pieces = [value[:rows]] + [
        swap(value[k * rows : (k + 1) * rows], k * high) for k in range(1, 4)
    ]
    moe_out = pl.pallas_call(
        sum_kernel,
        out_shape=jax.ShapeDtypeStruct((steps, rows_dev, width), jnp.bfloat16),
        in_specs=[VMEM] * 4,
        out_specs=VMEM,
        compiler_params=pltpu.CompilerParams(vmem_limit_bytes=4 * MIB),
        name="total",
    )(*pieces)

    heads = queries.shape[2]
    context = pl.pallas_call(
        attend_kernel,
        out_shape=jax.ShapeDtypeStruct((steps, rows_dev, heads, RANK), jnp.bfloat16),
        in_specs=[VMEM, VMEM, VMEM, SMEM],
        out_specs=VMEM,
        scratch_shapes=[pltpu.VMEM(latent_cache.shape[1:], jnp.bfloat16)],
        compiler_params=pltpu.CompilerParams(vmem_limit_bytes=16 * MIB),
        cost_estimate=pl.CostEstimate(
            flops=4 * rows_dev * steps * heads * latent_cache.shape[1] * latent_cache.shape[2],
            bytes_accessed=2 * (2 * queries.size + latent_cache.size),
            transcendentals=rows_dev * steps * heads * latent_cache.shape[1],
        ),
        name="attend",
    )(queries, latent_cache, new_latents, lengths)
    return (context, moe_out)


def solution(mesh):
    every = ("groups", "expert", "dp")
    routed = P(None, ("groups", "expert"), None)
    placed = (
        P(None, every, None, None),
        P(every, None, None),
        P(None, every, None),
        P(every),
        P(None, every, None),
        routed,
        routed,
        routed,
        P("expert", None, "dp"),
        P("expert", None, "dp"),
        P("expert", "dp", None),
        P(),
    )
    return jax.shard_map(
        per_device,
        mesh=mesh,
        in_specs=placed,
        out_specs=(P(None, every, None, None), P(None, every, None)),
        check_vma=False,
    )
```

```python
import functools

import jax
import jax.numpy as jnp
from jax import lax
from jax.experimental import pallas as pl
from jax.experimental.pallas import tpu as pltpu
from jax.sharding import PartitionSpec as P

RANK = 512
SCORE_SCALE = 0.07216878364870322
LANES = 128
PEERS = ("expert", "dp")
MIB = 1 << 20

VMEM = pl.BlockSpec(memory_space=pltpu.VMEM)
SMEM = pl.BlockSpec(memory_space=pltpu.SMEM)
HBM = pl.BlockSpec(memory_space=pltpu.HBM)
ANY = pl.BlockSpec(memory_space=pl.ANY)


def pack_kernel(experts, *refs):
    sources, out_ref, held, sems = refs[:5], refs[5], refs[6:11], refs[11]
    copies = [
        pltpu.make_async_copy(source, target, sems.at[i])
        for i, (source, target) in enumerate(zip(sources, held))
    ]
    for copy in copies:
        copy.start()
    for copy in copies:
        copy.wait()
    hidden_ref, first_ref, second_ref, weights_ref, hot_ref = held
    steps, rows_dev, width = hidden_ref.shape
    before, _, top = first_ref.shape
    tail = out_ref.shape[1] - width
    column = lax.broadcasted_iota(jnp.int32, (rows_dev, tail), 1)
    rows, marks = [], []
    for step in range(steps):
        if step < before:
            chosen = first_ref[step]
        else:
            chosen = second_ref[step - before]
            for replica in range(hot_ref.shape[0]):
                chosen = jnp.where(chosen == experts + replica, hot_ref[replica], chosen)
        weight = weights_ref[step]
        total = jnp.zeros((rows_dev, tail), jnp.float32)
        for k in range(top):
            picked = chosen[:, k : k + 1]
            here = (column == picked) | (column == picked + experts)
            total = total + jnp.where(here, weight[:, k : k + 1], 0.0)
        high = total.astype(jnp.bfloat16).astype(jnp.float32)
        rows.append(hidden_ref[step].astype(jnp.float32))
        marks.append(jnp.where(column < experts, high, total - high))
    out_ref[:, :width] = jnp.concatenate(rows, axis=0).astype(jnp.bfloat16)
    out_ref[:, width:] = jnp.concatenate(marks, axis=0).astype(jnp.bfloat16)


def load_kernel(*refs):
    count = len(refs) // 2
    copies = [
        pltpu.make_async_copy(refs[i], refs[count + i], refs[-1].at[i]) for i in range(count)
    ]
    for copy in copies:
        copy.start()
    for copy in copies:
        copy.wait()


def load(*arrays):
    return pl.pallas_call(
        load_kernel,
        out_shape=[jax.ShapeDtypeStruct(a.shape, a.dtype) for a in arrays],
        in_specs=[HBM] * len(arrays),
        out_specs=[VMEM] * len(arrays),
        scratch_shapes=[pltpu.SemaphoreType.DMA((len(arrays),))],
        compiler_params=pltpu.CompilerParams(vmem_limit_bytes=4 * MIB),
        cost_estimate=pl.CostEstimate(
            flops=0, bytes_accessed=sum(2 * a.size for a in arrays), transcendentals=0
        ),
        name="load",
    )(*(pltpu.with_memory_space_constraint(a, pltpu.HBM) for a in arrays))


def attend_kernel(
    queries_ref, cache_ref, new_ref, lengths_ref, down_hbm, out_ref, down_ref, keys, sem
):
    copy = pltpu.make_async_copy(down_hbm, down_ref, sem)
    copy.start()
    steps, rows_dev, heads, _ = queries_ref.shape
    slots = cache_ref.shape[2]
    fresh = [new_ref[t].astype(jnp.float32) for t in range(steps)]
    for b in range(rows_dev):
        rest = jnp.zeros((slots - steps, keys.shape[0]), jnp.float32)
        added = jnp.concatenate([rest] + [f[b : b + 1] for f in fresh], axis=0).astype(jnp.bfloat16)
        spot = lax.broadcasted_iota(jnp.int32, keys.shape, 1)
        keys[...] = jnp.where(spot < slots - steps, cache_ref[b], added.T)
        queries = queries_ref[:, b].reshape(steps * heads, queries_ref.shape[3])
        scores = jnp.dot(queries, keys[...], preferred_element_type=jnp.float32)
        scores = scores * SCORE_SCALE
        place = lax.broadcasted_iota(jnp.int32, scores.shape, 1)
        step = lax.broadcasted_iota(jnp.int32, scores.shape, 0) // heads
        age = place - (slots - steps)
        keep = (place < lengths_ref[b]) | ((age >= 0) & (age <= step))
        scores = jnp.where(keep, scores, -1e30)
        weight = jnp.exp(scores - jnp.max(scores, axis=1, keepdims=True))
        probs = weight / jnp.sum(weight, axis=1, keepdims=True)
        context = lax.dot_general(
            probs.astype(jnp.bfloat16),
            keys[:RANK],
            (((1,), (1,)), ((), ())),
            preferred_element_type=jnp.float32,
        )
        out_ref[:, b] = context.astype(jnp.bfloat16).reshape(steps, heads, RANK)
    copy.wait()


def expert_kernel(experts, tile, *refs):
    x_refs = refs[:4]
    gate, up, down, keep_ref, send_ref, x, hidden = refs[4:]
    width = down.shape[2]
    units = down.shape[1]
    parts = units // tile
    columns = width // parts
    piece = x_refs[0].shape[0]
    for i, x_ref in enumerate(x_refs):
        x[i * piece : (i + 1) * piece] = x_ref[...]
    own = lax.axis_index("expert")
    marks = x[:, width:].astype(jnp.float32)
    column = lax.broadcasted_iota(jnp.int32, marks.shape, 1)
    here = (column == own) | (column == own + experts)
    share = jnp.sum(jnp.where(here, marks, 0.0), axis=1, keepdims=True)
    for j in range(parts):
        cut = slice(j * tile, (j + 1) * tile)
        gate_act = jnp.dot(x[:, :width], gate[0, :, cut], preferred_element_type=jnp.float32)
        up_act = jnp.dot(x[:, :width], up[0, :, cut], preferred_element_type=jnp.float32)
        act = gate_act / (1.0 + jnp.exp(-gate_act)) * up_act
        hidden[:, cut] = act.astype(jnp.bfloat16)
    half = 2 * piece
    for j in range(parts):
        cut = slice(j * columns, (j + 1) * columns)
        out = jnp.dot(hidden[...], down[0, :, cut], preferred_element_type=jnp.float32) * share
        keep_ref[:, cut] = out[:half].astype(jnp.bfloat16)
        send_ref[:, cut] = out[half:].astype(jnp.bfloat16)


def join_kernel(*refs):
    *in_refs, out_ref = refs
    size = in_refs[0].shape[0]
    for i, ref in enumerate(in_refs):
        out_ref[i * size : (i + 1) * size] = ref[...]


def join(blocks):
    size, width = blocks[0].shape
    return pl.pallas_call(
        join_kernel,
        out_shape=jax.ShapeDtypeStruct((len(blocks) * size, width), blocks[0].dtype),
        in_specs=[VMEM] * len(blocks),
        out_specs=VMEM,
        compiler_params=pltpu.CompilerParams(vmem_limit_bytes=8 * MIB),
        name="join",
    )(*blocks)


def sum_kernel(*refs):
    *in_refs, out_ref = refs
    steps, rows_dev, _ = out_ref.shape
    total = in_refs[0][...].astype(jnp.float32)
    for ref in in_refs[1:]:
        total = total + ref[...].astype(jnp.float32)
    total = total.astype(jnp.bfloat16).astype(jnp.float32)
    for step in range(steps):
        out_ref[step] = total[step * rows_dev : (step + 1) * rows_dev].astype(jnp.bfloat16)


def swap(value, mask):
    size = lax.axis_size(PEERS)
    return lax.ppermute(value, PEERS, [(i, i ^ mask) for i in range(size)])


def per_device(
    queries,
    latent_cache,
    new_latents,
    lengths,
    hidden_in,
    first_routes,
    second_routes,
    route_weights,
    gate_weights,
    up_weights,
    down_weights,
    hot_experts,
):
    experts = lax.axis_size("expert")
    devices = lax.axis_size(PEERS)
    steps, rows_dev, width = hidden_in.shape
    rows = steps * rows_dev
    units = down_weights.shape[1]
    bits = devices.bit_length() - 1
    if first_routes.shape[1] != rows_dev:
        begin = lax.axis_index("dp") * rows_dev
        first_routes = lax.dynamic_slice_in_dim(first_routes, begin, rows_dev, 1)
        second_routes = lax.dynamic_slice_in_dim(second_routes, begin, rows_dev, 1)
        route_weights = lax.dynamic_slice_in_dim(route_weights, begin, rows_dev, 1)

    tail = -(-2 * experts // LANES) * LANES
    inputs = (hidden_in, first_routes, second_routes, route_weights)
    packed = pl.pallas_call(
        functools.partial(pack_kernel, experts),
        out_shape=jax.ShapeDtypeStruct((rows, width + tail), jnp.bfloat16),
        in_specs=[HBM] * 5,
        out_specs=VMEM,
        scratch_shapes=[pltpu.VMEM(a.shape, a.dtype) for a in inputs]
        + [pltpu.SMEM(hot_experts.shape, jnp.int32), pltpu.SemaphoreType.DMA((5,))],
        compiler_params=pltpu.CompilerParams(vmem_limit_bytes=4 * MIB),
        name="pack",
    )(*(pltpu.with_memory_space_constraint(a, pltpu.HBM) for a in (*inputs, hot_experts)))

    high = devices // 4
    packed, gate_weights, up_weights = lax.optimization_barrier((packed, gate_weights, up_weights))
    gate_loaded, up_loaded = load(gate_weights, up_weights)
    blocks = [packed] + [swap(packed, k * high) for k in range(1, 4)]
    held = join(blocks)
    for bit in range(bits - 3, 1, -1):
        held = join([held, swap(held, 1 << bit)])
    held, gate_loaded, up_loaded, lengths = lax.optimization_barrier(
        (held, gate_loaded, up_loaded, lengths)
    )
    second = swap(held, 2)
    heads = queries.shape[2]
    context, down_loaded = pl.pallas_call(
        attend_kernel,
        out_shape=[
            jax.ShapeDtypeStruct((steps, rows_dev, heads, RANK), jnp.bfloat16),
            jax.ShapeDtypeStruct(down_weights.shape, jnp.bfloat16),
        ],
        in_specs=[VMEM, VMEM, VMEM, SMEM, HBM],
        out_specs=[VMEM, VMEM],
        scratch_shapes=[pltpu.VMEM(latent_cache.shape[:0:-1], jnp.bfloat16), pltpu.SemaphoreType.DMA],
        compiler_params=pltpu.CompilerParams(vmem_limit_bytes=16 * MIB),
        cost_estimate=pl.CostEstimate(
            flops=4 * rows_dev * steps * heads * latent_cache.shape[1] * latent_cache.shape[2],
            bytes_accessed=2 * (2 * queries.size + latent_cache.size),
            transcendentals=rows_dev * steps * heads * latent_cache.shape[1],
        ),
        name="attend",
    )(
        queries,
        jnp.swapaxes(latent_cache, 1, 2),
        new_latents,
        lengths,
        pltpu.with_memory_space_constraint(down_weights, pltpu.HBM),
    )
    second, context, down_loaded = lax.optimization_barrier((second, context, down_loaded))
    other = swap(held, 1)
    other_second = swap(second, 1)

    count = 4 * held.shape[0]
    half = count // 2
    tile = min(256, units)
    parts = units // tile
    keep, send = pl.pallas_call(
        functools.partial(expert_kernel, experts, tile),
        out_shape=[jax.ShapeDtypeStruct((half, width), jnp.bfloat16)] * 2,
        in_specs=[VMEM] * 7,
        out_specs=[VMEM, VMEM],
        scratch_shapes=[
            pltpu.VMEM((count, width + tail), jnp.bfloat16),
            pltpu.VMEM((count, units), jnp.bfloat16),
        ],
        compiler_params=pltpu.CompilerParams(vmem_limit_bytes=24 * MIB),
        cost_estimate=pl.CostEstimate(
            flops=6 * count * width * units,
            bytes_accessed=6 * width * units,
            transcendentals=count * units,
        ),
        name="experts",
    )(
        held,
        second,
        other,
        other_second,
        gate_loaded,
        up_loaded,
        down_loaded,
    )

    back = swap(send, 1)
    value = keep.astype(jnp.float32) + back.astype(jnp.float32)
    for bit in range(1, bits - 2):
        size = value.shape[0] // 2
        back = swap(value[size:].astype(jnp.bfloat16), 1 << bit)
        value = value[:size] + back.astype(jnp.float32)
    value = value.astype(jnp.bfloat16)
    pieces = [value[:rows]] + [
        swap(value[k * rows : (k + 1) * rows], k * high) for k in range(1, 4)
    ]
    moe_out = pl.pallas_call(
        sum_kernel,
        out_shape=jax.ShapeDtypeStruct((steps, rows_dev, width), jnp.bfloat16),
        in_specs=[VMEM] * 4,
        out_specs=VMEM,
        compiler_params=pltpu.CompilerParams(vmem_limit_bytes=4 * MIB),
        name="total",
    )(*pieces)

    return (context, moe_out)


def solution(mesh):
    every = ("groups", "expert", "dp")
    routed = P(None, ("groups", "expert"), None)
    placed = (
        P(None, every, None, None),
        P(every, None, None),
        P(None, every, None),
        P(every),
        P(None, every, None),
        routed,
        routed,
        routed,
        P("expert", None, "dp"),
        P("expert", None, "dp"),
        P("expert", "dp", None),
        P(),
    )
    return jax.shard_map(
        per_device,
        mesh=mesh,
        in_specs=placed,
        out_specs=(P(None, every, None, None), P(None, every, None)),
        check_vma=False,
    )
```

```python
import functools

import jax
import jax.numpy as jnp
from jax import lax
from jax.experimental import pallas as pl
from jax.experimental.pallas import tpu as pltpu
from jax.sharding import PartitionSpec as P

RANK = 512
SCORE_SCALE = 0.07216878364870322
LANES = 128
PEERS = ("expert", "dp")
MIB = 1 << 20

VMEM = pl.BlockSpec(memory_space=pltpu.VMEM)
SMEM = pl.BlockSpec(memory_space=pltpu.SMEM)
HBM = pl.BlockSpec(memory_space=pltpu.HBM)
ANY = pl.BlockSpec(memory_space=pl.ANY)


def pack_kernel(experts, *refs):
    sources, out_ref, held, sems = refs[:5], refs[5], refs[6:11], refs[11]
    copies = [
        pltpu.make_async_copy(source, target, sems.at[i])
        for i, (source, target) in enumerate(zip(sources, held))
    ]
    for copy in copies:
        copy.start()
    for copy in copies:
        copy.wait()
    hidden_ref, first_ref, second_ref, weights_ref, hot_ref = held
    steps, rows_dev, width = hidden_ref.shape
    before, _, top = first_ref.shape
    tail = out_ref.shape[1] - width
    column = lax.broadcasted_iota(jnp.int32, (rows_dev, tail), 1)
    rows, marks = [], []
    for step in range(steps):
        if step < before:
            chosen = first_ref[step]
        else:
            chosen = second_ref[step - before]
            for replica in range(hot_ref.shape[0]):
                chosen = jnp.where(chosen == experts + replica, hot_ref[replica], chosen)
        weight = weights_ref[step]
        total = jnp.zeros((rows_dev, tail), jnp.float32)
        for k in range(top):
            picked = chosen[:, k : k + 1]
            here = (column == picked) | (column == picked + experts)
            total = total + jnp.where(here, weight[:, k : k + 1], 0.0)
        high = total.astype(jnp.bfloat16).astype(jnp.float32)
        rows.append(hidden_ref[step].astype(jnp.float32))
        marks.append(jnp.where(column < experts, high, total - high))
    out_ref[:, :width] = jnp.concatenate(rows, axis=0).astype(jnp.bfloat16)
    out_ref[:, width:] = jnp.concatenate(marks, axis=0).astype(jnp.bfloat16)


def attend_kernel(queries_ref, cache_ref, new_ref, lengths_ref, out_ref, keys):
    steps, rows_dev, heads, _ = queries_ref.shape
    slots = cache_ref.shape[2]
    fresh = [new_ref[t].astype(jnp.float32) for t in range(steps)]
    for b in range(rows_dev):
        rest = jnp.zeros((slots - steps, keys.shape[0]), jnp.float32)
        added = jnp.concatenate([rest] + [f[b : b + 1] for f in fresh], axis=0).astype(jnp.bfloat16)
        spot = lax.broadcasted_iota(jnp.int32, keys.shape, 1)
        keys[...] = jnp.where(spot < slots - steps, cache_ref[b], added.T)
        queries = queries_ref[:, b].reshape(steps * heads, queries_ref.shape[3])
        scores = jnp.dot(queries, keys[...], preferred_element_type=jnp.float32)
        scores = scores * SCORE_SCALE
        place = lax.broadcasted_iota(jnp.int32, scores.shape, 1)
        step = lax.broadcasted_iota(jnp.int32, scores.shape, 0) // heads
        age = place - (slots - steps)
        keep = (place < lengths_ref[b]) | ((age >= 0) & (age <= step))
        scores = jnp.where(keep, scores, -1e30)
        weight = jnp.exp(scores - jnp.max(scores, axis=1, keepdims=True))
        probs = weight / jnp.sum(weight, axis=1, keepdims=True)
        context = lax.dot_general(
            probs.astype(jnp.bfloat16),
            keys[:RANK],
            (((1,), (1,)), ((), ())),
            preferred_element_type=jnp.float32,
        )
        out_ref[:, b] = context.astype(jnp.bfloat16).reshape(steps, heads, RANK)


def expert_kernel(experts, tile, pieces, *refs):
    x_refs, refs = refs[:pieces], refs[pieces:]
    gate, up, down, keep_far, send_far, keep_near, send_near, x, hidden = refs
    width = down.shape[2]
    units = down.shape[1]
    parts = units // tile
    columns = width // parts
    piece = x_refs[0].shape[0]
    for i, x_ref in enumerate(x_refs):
        x[i * piece : (i + 1) * piece] = x_ref[...]
    own = lax.axis_index("expert")
    marks = x[:, width:].astype(jnp.float32)
    column = lax.broadcasted_iota(jnp.int32, marks.shape, 1)
    here = (column == own) | (column == own + experts)
    share = jnp.sum(jnp.where(here, marks, 0.0), axis=1, keepdims=True)
    for j in range(parts):
        cut = slice(j * tile, (j + 1) * tile)
        gate_act = jnp.dot(x[:, :width], gate[0, :, cut], preferred_element_type=jnp.float32)
        up_act = jnp.dot(x[:, :width], up[0, :, cut], preferred_element_type=jnp.float32)
        act = gate_act / (1.0 + jnp.exp(-gate_act)) * up_act
        hidden[:, cut] = act.astype(jnp.bfloat16)
    quarter = keep_far.shape[0]
    for j in range(parts):
        cut = slice(j * columns, (j + 1) * columns)
        out = jnp.dot(hidden[...], down[0, :, cut], preferred_element_type=jnp.float32) * share
        for i, ref in enumerate((keep_near, keep_far, send_near, send_far)):
            ref[:, cut] = out[i * quarter : (i + 1) * quarter].astype(jnp.bfloat16)


def join_kernel(*refs):
    *in_refs, out_ref = refs
    size = in_refs[0].shape[0]
    for i, ref in enumerate(in_refs):
        out_ref[i * size : (i + 1) * size] = ref[...]


def join(blocks):
    size, width = blocks[0].shape
    return pl.pallas_call(
        join_kernel,
        out_shape=jax.ShapeDtypeStruct((len(blocks) * size, width), blocks[0].dtype),
        in_specs=[VMEM] * len(blocks),
        out_specs=VMEM,
        compiler_params=pltpu.CompilerParams(vmem_limit_bytes=8 * MIB),
        cost_estimate=pl.CostEstimate(flops=10000000000, bytes_accessed=0, transcendentals=0),
        name="join",
    )(*blocks)


def sum_kernel(*refs):
    *in_refs, out_ref = refs
    steps, rows_dev, _ = out_ref.shape
    total = in_refs[0][...].astype(jnp.float32)
    for ref in in_refs[1:]:
        total = total + ref[...].astype(jnp.float32)
    total = total.astype(jnp.bfloat16).astype(jnp.float32)
    for step in range(steps):
        out_ref[step] = total[step * rows_dev : (step + 1) * rows_dev].astype(jnp.bfloat16)


def swap(value, mask):
    size = lax.axis_size(PEERS)
    return lax.ppermute(value, PEERS, [(i, i ^ mask) for i in range(size)])


def add(*values):
    total = values[0].astype(jnp.float32)
    for value in values[1:]:
        total = total + value.astype(jnp.float32)
    return total.astype(jnp.bfloat16)


def per_device(
    queries,
    latent_cache,
    new_latents,
    lengths,
    hidden_in,
    first_routes,
    second_routes,
    route_weights,
    gate_weights,
    up_weights,
    down_weights,
    hot_experts,
):
    experts = lax.axis_size("expert")
    devices = lax.axis_size(PEERS)
    steps, rows_dev, width = hidden_in.shape
    rows = steps * rows_dev
    units = down_weights.shape[1]
    bits = devices.bit_length() - 1
    if first_routes.shape[1] != rows_dev:
        begin = lax.axis_index("dp") * rows_dev
        first_routes = lax.dynamic_slice_in_dim(first_routes, begin, rows_dev, 1)
        second_routes = lax.dynamic_slice_in_dim(second_routes, begin, rows_dev, 1)
        route_weights = lax.dynamic_slice_in_dim(route_weights, begin, rows_dev, 1)

    tail = -(-2 * experts // LANES) * LANES
    inputs = (hidden_in, first_routes, second_routes, route_weights)
    packed = pl.pallas_call(
        functools.partial(pack_kernel, experts),
        out_shape=jax.ShapeDtypeStruct((rows, width + tail), jnp.bfloat16),
        in_specs=[HBM] * 5,
        out_specs=VMEM,
        scratch_shapes=[pltpu.VMEM(a.shape, a.dtype) for a in inputs]
        + [pltpu.SMEM(hot_experts.shape, jnp.int32), pltpu.SemaphoreType.DMA((5,))],
        compiler_params=pltpu.CompilerParams(vmem_limit_bytes=4 * MIB),
        name="pack",
    )(*(pltpu.with_memory_space_constraint(a, pltpu.HBM) for a in (*inputs, hot_experts)))

    high = devices // 4
    base = packed
    for bit in range(2, bits - 2):
        base = join([base, swap(base, 1 << bit)])
    size = base.shape[0]
    third = swap(base, 3 * high)
    second = swap(base, 2 * high)
    first = swap(base, high)
    near = join([base, first])
    far = join([second, third])
    near_y = swap(near, 2)
    far_y = swap(far, 2)
    parts = [near, far, near_y, far_y]
    parts = parts + [swap(part, 1) for part in parts]

    count = 16 * size
    tile = min(256, units)
    half = jax.ShapeDtypeStruct((4 * size, width), jnp.bfloat16)
    keep_far, send_far, keep_near, send_near = pl.pallas_call(
        functools.partial(expert_kernel, experts, tile, len(parts)),
        out_shape=[half] * 4,
        in_specs=[VMEM] * (len(parts) + 3),
        out_specs=[VMEM] * 4,
        scratch_shapes=[
            pltpu.VMEM((count, width + tail), jnp.bfloat16),
            pltpu.VMEM((count, units), jnp.bfloat16),
        ],
        compiler_params=pltpu.CompilerParams(vmem_limit_bytes=24 * MIB),
        cost_estimate=pl.CostEstimate(
            flops=6 * count * width * units,
            bytes_accessed=6 * width * units,
            transcendentals=count * units,
        ),
        name="experts",
    )(*parts, gate_weights, up_weights, down_weights)

    far = add(keep_far, swap(send_far, 1))
    near = add(keep_near, swap(send_near, 1))
    far_third, far_second, far_first = far[3 * size :], far[2 * size : 3 * size], far[: 2 * size]
    far_third, lengths = lax.optimization_barrier((far_third, lengths))
    third = swap(far_third, 2)
    second = swap(far_second, 2)
    first = swap(far_first, 2)
    heads = queries.shape[2]
    context = pl.pallas_call(
        attend_kernel,
        out_shape=jax.ShapeDtypeStruct((steps, rows_dev, heads, RANK), jnp.bfloat16),
        in_specs=[VMEM, VMEM, VMEM, SMEM],
        out_specs=VMEM,
        scratch_shapes=[pltpu.VMEM(latent_cache.shape[:0:-1], jnp.bfloat16)],
        compiler_params=pltpu.CompilerParams(vmem_limit_bytes=16 * MIB),
        cost_estimate=pl.CostEstimate(
            flops=4 * rows_dev * steps * heads * latent_cache.shape[1] * latent_cache.shape[2],
            bytes_accessed=2 * (2 * queries.size + latent_cache.size),
            transcendentals=rows_dev * steps * heads * latent_cache.shape[1],
        ),
        name="attend",
    )(
        queries,
        jnp.swapaxes(latent_cache, 1, 2),
        new_latents,
        lengths,
    )
    first, context = lax.optimization_barrier((first, context))
    third = swap(add(near[3 * size :], third), 3 * high)
    second = swap(add(near[2 * size : 3 * size], second), 2 * high)
    total = add(near[: 2 * size], first)
    pieces = [total[:size], swap(total[size:], high), second, third]
    for bit in range(bits - 3, 1, -1):
        value = add(*pieces)
        middle = value.shape[0] // 2
        pieces = [value[:middle], swap(value[middle:], 1 << bit)]
    moe_out = pl.pallas_call(
        sum_kernel,
        out_shape=jax.ShapeDtypeStruct((steps, rows_dev, width), jnp.bfloat16),
        in_specs=[VMEM] * len(pieces),
        out_specs=VMEM,
        compiler_params=pltpu.CompilerParams(vmem_limit_bytes=4 * MIB),
        name="total",
    )(*pieces)
    return (context, moe_out)


def solution(mesh):
    every = ("groups", "expert", "dp")
    routed = P(None, ("groups", "expert"), None)
    placed = (
        P(None, every, None, None),
        P(every, None, None),
        P(None, every, None),
        P(every),
        P(None, every, None),
        routed,
        routed,
        routed,
        P("expert", None, "dp"),
        P("expert", None, "dp"),
        P("expert", "dp", None),
        P(),
    )
    return jax.shard_map(
        per_device,
        mesh=mesh,
        in_specs=placed,
        out_specs=(P(None, every, None, None), P(None, every, None)),
        check_vma=False,
    )
```

```python
import functools

import jax
import jax.numpy as jnp
from jax import lax
from jax.experimental import pallas as pl
from jax.experimental.pallas import tpu as pltpu
from jax.sharding import PartitionSpec as P

RANK = 512
SCORE_SCALE = 0.07216878364870322
LANES = 128
SUBLANES = 8
PEERS = ("expert", "dp")
MIB = 1 << 20

VMEM = pl.BlockSpec(memory_space=pltpu.VMEM)
SMEM = pl.BlockSpec(memory_space=pltpu.SMEM)
HBM = pl.BlockSpec(memory_space=pltpu.HBM)
ANY = pl.BlockSpec(memory_space=pl.ANY)


def pack_kernel(experts, *refs):
    sources, out_ref, held, sems = refs[:5], refs[5], refs[6:11], refs[11]
    copies = [
        pltpu.make_async_copy(source, target, sems.at[i])
        for i, (source, target) in enumerate(zip(sources, held))
    ]
    for copy in copies:
        copy.start()
    for copy in copies:
        copy.wait()
    hidden_ref, first_ref, second_ref, weights_ref, hot_ref = held
    steps, rows_dev, width = hidden_ref.shape
    before, _, top = first_ref.shape
    tail = out_ref.shape[1] - width
    column = lax.broadcasted_iota(jnp.int32, (rows_dev, tail), 1)
    rows, marks = [], []
    for step in range(steps):
        if step < before:
            chosen = first_ref[step]
        else:
            chosen = second_ref[step - before]
            for replica in range(hot_ref.shape[0]):
                chosen = jnp.where(chosen == experts + replica, hot_ref[replica], chosen)
        weight = weights_ref[step]
        total = jnp.zeros((rows_dev, tail), jnp.float32)
        for k in range(top):
            picked = chosen[:, k : k + 1]
            here = (column == picked) | (column == picked + experts)
            total = total + jnp.where(here, weight[:, k : k + 1], 0.0)
        high = total.astype(jnp.bfloat16).astype(jnp.float32)
        rows.append(hidden_ref[step].astype(jnp.float32))
        marks.append(jnp.where(column < experts, high, total - high))
    out_ref[:, :width] = jnp.concatenate(rows, axis=0).astype(jnp.bfloat16)
    out_ref[:, width:] = jnp.concatenate(marks, axis=0).astype(jnp.bfloat16)


def attend_kernel(queries_ref, cache_ref, new_ref, lengths_ref, out_hbm, keys, context, sems):
    steps, rows_dev, heads, _ = queries_ref.shape
    slots = cache_ref.shape[2]
    whole = slots - LANES
    fresh = [new_ref[t].astype(jnp.float32) for t in range(steps)]
    spare = jnp.zeros((SUBLANES - steps, keys.shape[1]), jnp.float32)
    target = lax.broadcasted_iota(jnp.int32, (SUBLANES, LANES), 1) - (LANES - steps)
    source = lax.broadcasted_iota(jnp.int32, (SUBLANES, LANES), 0)
    spots = jnp.where(target == source, 1.0, 0.0).astype(jnp.bfloat16)
    spot = lax.broadcasted_iota(jnp.int32, (keys.shape[1], LANES), 1)
    place = lax.broadcasted_iota(jnp.int32, (steps * heads, slots), 1)
    step = lax.broadcasted_iota(jnp.int32, (steps * heads, slots), 0) // heads
    age = place - (slots - steps)
    recent = (age >= 0) & (age <= step)
    copies = []
    for b in range(rows_dev):
        added = jnp.concatenate([f[b : b + 1] for f in fresh] + [spare], axis=0)
        added = lax.dot_general(
            added.astype(jnp.bfloat16),
            spots,
            (((0,), (0,)), ((), ())),
            preferred_element_type=jnp.float32,
        ).astype(jnp.bfloat16)
        keys[b, :, 0:whole] = cache_ref[b, :, 0:whole]
        keys[b, :, whole:] = jnp.where(spot < LANES - steps, cache_ref[b, :, whole:], added)
    scores = []
    for b in range(rows_dev):
        queries = queries_ref[:, b].reshape(steps * heads, queries_ref.shape[3])
        raw = jnp.dot(queries, keys[b], preferred_element_type=jnp.float32)
        scores.append(jnp.where((place < lengths_ref[b]) | recent, raw * SCORE_SCALE, -1e30))
    for b in range(rows_dev):
        weight = jnp.exp(scores[b] - jnp.max(scores[b], axis=1, keepdims=True))
        probs = weight * (1.0 / jnp.sum(weight, axis=1, keepdims=True))
        result = lax.dot_general(
            probs.astype(jnp.bfloat16),
            keys[b, :RANK],
            (((1,), (1,)), ((), ())),
            preferred_element_type=jnp.float32,
        )
        context[:, b] = result.astype(jnp.bfloat16).reshape(steps, heads, RANK)
        copies.append(pltpu.make_async_copy(context.at[:, b], out_hbm.at[:, b], sems.at[b]))
        copies[b].start()
    for copy in copies:
        copy.wait()


def expert_kernel(experts, tile, pieces, *refs):
    x_refs, refs = refs[:pieces], refs[pieces:]
    gate, up, down, keep_far, send_far, keep_near, send_near, x, hidden = refs
    width = down.shape[2]
    units = down.shape[1]
    parts = units // tile
    columns = width // parts
    row = 0
    for x_ref in x_refs:
        x[row : row + x_ref.shape[0]] = x_ref[...]
        row += x_ref.shape[0]
    own = lax.axis_index("expert")
    marks = x[:, width:].astype(jnp.float32)
    column = lax.broadcasted_iota(jnp.int32, marks.shape, 1)
    here = (column == own) | (column == own + experts)
    share = jnp.sum(jnp.where(here, marks, 0.0), axis=1, keepdims=True)
    for j in range(parts):
        cut = slice(j * tile, (j + 1) * tile)
        gate_act = jnp.dot(x[:, :width], gate[0, :, cut], preferred_element_type=jnp.float32)
        up_act = jnp.dot(x[:, :width], up[0, :, cut], preferred_element_type=jnp.float32)
        act = gate_act / (1.0 + jnp.exp(-gate_act)) * up_act
        hidden[:, cut] = act.astype(jnp.bfloat16)
    quarter = keep_far.shape[0]
    for j in range(parts):
        cut = slice(j * columns, (j + 1) * columns)
        out = jnp.dot(hidden[...], down[0, :, cut], preferred_element_type=jnp.float32) * share
        for i, ref in enumerate((keep_near, keep_far, send_near, send_far)):
            ref[:, cut] = out[i * quarter : (i + 1) * quarter].astype(jnp.bfloat16)


def join_kernel(*refs):
    *in_refs, out_ref = refs
    size = in_refs[0].shape[0]
    for i, ref in enumerate(in_refs):
        out_ref[i * size : (i + 1) * size] = ref[...]


def join(blocks):
    size, width = blocks[0].shape
    return pl.pallas_call(
        join_kernel,
        out_shape=jax.ShapeDtypeStruct((len(blocks) * size, width), blocks[0].dtype),
        in_specs=[VMEM] * len(blocks),
        out_specs=VMEM,
        compiler_params=pltpu.CompilerParams(vmem_limit_bytes=8 * MIB),
        cost_estimate=pl.CostEstimate(flops=10000000000, bytes_accessed=0, transcendentals=0),
        name="join",
    )(*blocks)


def sum_kernel(*refs):
    *in_refs, out_ref = refs
    steps, rows_dev, _ = out_ref.shape
    total = in_refs[0][...].astype(jnp.float32)
    for ref in in_refs[1:]:
        total = total + ref[...].astype(jnp.float32)
    total = total.astype(jnp.bfloat16).astype(jnp.float32)
    for step in range(steps):
        out_ref[step] = total[step * rows_dev : (step + 1) * rows_dev].astype(jnp.bfloat16)


def swap(value, mask):
    size = lax.axis_size(PEERS)
    return lax.ppermute(value, PEERS, [(i, i ^ mask) for i in range(size)])


def add(*values):
    total = values[0].astype(jnp.float32)
    for value in values[1:]:
        total = total + value.astype(jnp.float32)
    return total.astype(jnp.bfloat16)


def per_device(
    queries,
    latent_cache,
    new_latents,
    lengths,
    hidden_in,
    first_routes,
    second_routes,
    route_weights,
    gate_weights,
    up_weights,
    down_weights,
    hot_experts,
):
    experts = lax.axis_size("expert")
    devices = lax.axis_size(PEERS)
    steps, rows_dev, width = hidden_in.shape
    rows = steps * rows_dev
    units = down_weights.shape[1]
    bits = devices.bit_length() - 1
    if first_routes.shape[1] != rows_dev:
        begin = lax.axis_index("dp") * rows_dev
        first_routes = lax.dynamic_slice_in_dim(first_routes, begin, rows_dev, 1)
        second_routes = lax.dynamic_slice_in_dim(second_routes, begin, rows_dev, 1)
        route_weights = lax.dynamic_slice_in_dim(route_weights, begin, rows_dev, 1)

    tail = -(-2 * experts // LANES) * LANES
    inputs = (hidden_in, first_routes, second_routes, route_weights)
    packed = pl.pallas_call(
        functools.partial(pack_kernel, experts),
        out_shape=jax.ShapeDtypeStruct((rows, width + tail), jnp.bfloat16),
        in_specs=[HBM] * 5,
        out_specs=VMEM,
        scratch_shapes=[pltpu.VMEM(a.shape, a.dtype) for a in inputs]
        + [pltpu.SMEM(hot_experts.shape, jnp.int32), pltpu.SemaphoreType.DMA((5,))],
        compiler_params=pltpu.CompilerParams(vmem_limit_bytes=4 * MIB),
        name="pack",
    )(*(pltpu.with_memory_space_constraint(a, pltpu.HBM) for a in (*inputs, hot_experts)))

    high = devices // 4
    base = packed
    for bit in range(2, bits - 2):
        base = join([base, swap(base, 1 << bit)])
    size = base.shape[0]
    third = swap(base, 2 * high)
    second = swap(base, 3 * high)
    first = swap(base, 1 * high)
    near = join([base, first])
    far = join([second, third])
    near_y = swap(near, 2)
    far_y = swap(far, 2)
    parts = [near, far, near_y, far_y]
    parts = parts + [swap(part, 1) for part in parts]

    count = 16 * size
    tile = min(256, units)
    half = jax.ShapeDtypeStruct((4 * size, width), jnp.bfloat16)
    keep_far, send_far, keep_near, send_near = pl.pallas_call(
        functools.partial(expert_kernel, experts, tile, len(parts)),
        out_shape=[half] * 4,
        in_specs=[VMEM] * (len(parts) + 3),
        out_specs=[VMEM] * 4,
        scratch_shapes=[
            pltpu.VMEM((count, width + tail), jnp.bfloat16),
            pltpu.VMEM((count, units), jnp.bfloat16),
        ],
        compiler_params=pltpu.CompilerParams(vmem_limit_bytes=24 * MIB),
        cost_estimate=pl.CostEstimate(
            flops=6 * count * width * units,
            bytes_accessed=6 * width * units,
            transcendentals=count * units,
        ),
        name="experts",
    )(*parts, gate_weights, up_weights, down_weights)

    far = add(keep_far, swap(send_far, 1))
    near = add(keep_near, swap(send_near, 1))
    far_third, far_second, far_first = far[3 * size :], far[2 * size : 3 * size], far[: 2 * size]
    far_third, lengths = lax.optimization_barrier((far_third, lengths))
    third = swap(far_third, 2)
    second = swap(far_second, 2)
    first = swap(far_first, 2)
    heads = queries.shape[2]
    context = pl.pallas_call(
        attend_kernel,
        out_shape=jax.ShapeDtypeStruct((steps, rows_dev, heads, RANK), jnp.bfloat16),
        in_specs=[VMEM, VMEM, VMEM, SMEM],
        out_specs=HBM,
        scratch_shapes=[
            pltpu.VMEM(
                (rows_dev, latent_cache.shape[2], latent_cache.shape[1]), jnp.bfloat16
            ),
            pltpu.VMEM((steps, rows_dev, heads, RANK), jnp.bfloat16),
            pltpu.SemaphoreType.DMA((rows_dev,)),
        ],
        compiler_params=pltpu.CompilerParams(vmem_limit_bytes=16 * MIB),
        cost_estimate=pl.CostEstimate(
            flops=4 * rows_dev * steps * heads * latent_cache.shape[1] * latent_cache.shape[2],
            bytes_accessed=2 * (2 * queries.size + latent_cache.size),
            transcendentals=rows_dev * steps * heads * latent_cache.shape[1],
        ),
        name="attend",
    )(
        queries,
        jnp.swapaxes(latent_cache, 1, 2),
        new_latents,
        lengths,
    )
    first, context = lax.optimization_barrier((first, context))
    third = swap(add(near[3 * size :], third), 2 * high)
    second = swap(add(near[2 * size : 3 * size], second), 3 * high)
    total = add(near[: 2 * size], first)
    pieces = [total[:size], swap(total[size:], 1 * high), second, third]
    for bit in range(bits - 3, 1, -1):
        value = add(*pieces)
        middle = value.shape[0] // 2
        pieces = [value[:middle], swap(value[middle:], 1 << bit)]
    moe_out = pl.pallas_call(
        sum_kernel,
        out_shape=jax.ShapeDtypeStruct((steps, rows_dev, width), jnp.bfloat16),
        in_specs=[VMEM] * len(pieces),
        out_specs=VMEM,
        compiler_params=pltpu.CompilerParams(vmem_limit_bytes=4 * MIB),
        name="total",
    )(*pieces)
    return (context, moe_out)


def solution(mesh):
    every = ("groups", "expert", "dp")
    routed = P(None, ("groups", "expert"), None)
    placed = (
        P(None, every, None, None),
        P(every, None, None),
        P(None, every, None),
        P(every),
        P(None, every, None),
        routed,
        routed,
        routed,
        P("expert", None, "dp"),
        P("expert", None, "dp"),
        P("expert", "dp", None),
        P(),
    )
    return jax.shard_map(
        per_device,
        mesh=mesh,
        in_specs=placed,
        out_specs=(P(None, every, None, None), P(None, every, None)),
        check_vma=False,
    )
```

```python
import functools

import jax
import jax.numpy as jnp
from jax import lax
from jax.experimental import pallas as pl
from jax.experimental.pallas import tpu as pltpu
from jax.sharding import PartitionSpec as P

RANK = 512
SCORE_SCALE = 0.07216878364870322
LANES = 128
SUBLANES = 8
PEERS = ("expert", "dp")
MIB = 1 << 20

VMEM = pl.BlockSpec(memory_space=pltpu.VMEM)
SMEM = pl.BlockSpec(memory_space=pltpu.SMEM)
HBM = pl.BlockSpec(memory_space=pltpu.HBM)
ANY = pl.BlockSpec(memory_space=pl.ANY)


def pack_kernel(experts, *refs):
    sources, out_ref, held, sems = refs[:5], refs[5], refs[6:11], refs[11]
    copies = [
        pltpu.make_async_copy(source, target, sems.at[i])
        for i, (source, target) in enumerate(zip(sources, held))
    ]
    for copy in copies:
        copy.start()
    for copy in copies:
        copy.wait()
    hidden_ref, first_ref, second_ref, weights_ref, hot_ref = held
    steps, rows_dev, width = hidden_ref.shape
    before, _, top = first_ref.shape
    tail = out_ref.shape[1] - width
    column = lax.broadcasted_iota(jnp.int32, (rows_dev, tail), 1)
    rows, marks = [], []
    for step in range(steps):
        if step < before:
            chosen = first_ref[step]
        else:
            chosen = second_ref[step - before]
            for replica in range(hot_ref.shape[0]):
                chosen = jnp.where(chosen == experts + replica, hot_ref[replica], chosen)
        weight = weights_ref[step]
        total = jnp.zeros((rows_dev, tail), jnp.float32)
        for k in range(top):
            picked = chosen[:, k : k + 1]
            here = (column == picked) | (column == picked + experts)
            total = total + jnp.where(here, weight[:, k : k + 1], 0.0)
        high = total.astype(jnp.bfloat16).astype(jnp.float32)
        rows.append(hidden_ref[step].astype(jnp.float32))
        marks.append(jnp.where(column < experts, high, total - high))
    out_ref[:, :width] = jnp.concatenate(rows, axis=0).astype(jnp.bfloat16)
    out_ref[:, width:] = jnp.concatenate(marks, axis=0).astype(jnp.bfloat16)


def attend_kernel(queries_ref, cache_ref, new_ref, lengths_ref, out_hbm, keys, context, sems):
    steps, rows_dev, heads, _ = queries_ref.shape
    slots = cache_ref.shape[2]
    whole = slots - LANES
    fresh = [new_ref[t].astype(jnp.float32) for t in range(steps)]
    spare = jnp.zeros((SUBLANES - steps, keys.shape[1]), jnp.float32)
    target = lax.broadcasted_iota(jnp.int32, (SUBLANES, LANES), 1) - (LANES - steps)
    source = lax.broadcasted_iota(jnp.int32, (SUBLANES, LANES), 0)
    spots = jnp.where(target == source, 1.0, 0.0).astype(jnp.bfloat16)
    spot = lax.broadcasted_iota(jnp.int32, (keys.shape[1], LANES), 1)
    place = lax.broadcasted_iota(jnp.int32, (steps * heads, slots), 1)
    step = lax.broadcasted_iota(jnp.int32, (steps * heads, slots), 0) // heads
    age = place - (slots - steps)
    recent = (age >= 0) & (age <= step)
    copies = []
    for b in range(rows_dev):
        added = jnp.concatenate([f[b : b + 1] for f in fresh] + [spare], axis=0)
        added = lax.dot_general(
            added.astype(jnp.bfloat16),
            spots,
            (((0,), (0,)), ((), ())),
            preferred_element_type=jnp.float32,
        ).astype(jnp.bfloat16)
        keys[b, :, 0:whole] = cache_ref[b, :, 0:whole]
        keys[b, :, whole:] = jnp.where(spot < LANES - steps, cache_ref[b, :, whole:], added)
    scores = []
    for b in range(rows_dev):
        queries = queries_ref[:, b].reshape(steps * heads, queries_ref.shape[3])
        raw = jnp.dot(queries, keys[b], preferred_element_type=jnp.float32)
        scores.append(jnp.where((place < lengths_ref[b]) | recent, raw * SCORE_SCALE, -1e30))
    for b in range(rows_dev):
        weight = jnp.exp(scores[b] - jnp.max(scores[b], axis=1, keepdims=True))
        probs = weight * (1.0 / jnp.sum(weight, axis=1, keepdims=True))
        result = lax.dot_general(
            probs.astype(jnp.bfloat16),
            keys[b, :RANK],
            (((1,), (1,)), ((), ())),
            preferred_element_type=jnp.float32,
        )
        context[:, b] = result.astype(jnp.bfloat16).reshape(steps, heads, RANK)
        copies.append(pltpu.make_async_copy(context.at[:, b], out_hbm.at[:, b], sems.at[b]))
        copies[b].start()
    for copy in copies:
        copy.wait()


def expert_kernel(experts, tile, pieces, *refs):
    x_refs, refs = refs[:pieces], refs[pieces:]
    gate, up, down, keep_far, send_far, keep_near, send_near, x, hidden = refs
    width = down.shape[2]
    units = down.shape[1]
    parts = units // tile
    columns = width // parts
    row = 0
    for x_ref in x_refs:
        x[row : row + x_ref.shape[0]] = x_ref[...]
        row += x_ref.shape[0]
    own = lax.axis_index("expert")
    marks = x[:, width:].astype(jnp.float32)
    column = lax.broadcasted_iota(jnp.int32, marks.shape, 1)
    here = (column == own) | (column == own + experts)
    share = jnp.sum(jnp.where(here, marks, 0.0), axis=1, keepdims=True)
    for j in range(parts):
        cut = slice(j * tile, (j + 1) * tile)
        gate_act = jnp.dot(x[:, :width], gate[0, :, cut], preferred_element_type=jnp.float32)
        up_act = jnp.dot(x[:, :width], up[0, :, cut], preferred_element_type=jnp.float32)
        act = gate_act / (1.0 + jnp.exp(-gate_act)) * up_act
        hidden[:, cut] = act.astype(jnp.bfloat16)
    quarter = keep_far.shape[0]
    for j in range(parts):
        cut = slice(j * columns, (j + 1) * columns)
        out = jnp.dot(hidden[...], down[0, :, cut], preferred_element_type=jnp.float32) * share
        for i, ref in enumerate((keep_near, keep_far, send_near, send_far)):
            ref[:, cut] = out[i * quarter : (i + 1) * quarter].astype(jnp.bfloat16)


def join_kernel(*refs):
    *in_refs, out_ref = refs
    blocks = [ref[...].astype(jnp.float32) for ref in in_refs]
    out_ref[...] = jnp.concatenate(blocks, axis=0).astype(jnp.bfloat16)


def join(blocks):
    size, width = blocks[0].shape
    return pl.pallas_call(
        join_kernel,
        out_shape=jax.ShapeDtypeStruct((len(blocks) * size, width), blocks[0].dtype),
        in_specs=[VMEM] * len(blocks),
        out_specs=VMEM,
        compiler_params=pltpu.CompilerParams(vmem_limit_bytes=8 * MIB),
        cost_estimate=pl.CostEstimate(flops=10000000000, bytes_accessed=0, transcendentals=0),
        name="join",
    )(*blocks)


def sum_kernel(*refs):
    *in_refs, out_ref = refs
    steps, rows_dev, _ = out_ref.shape
    total = in_refs[0][...].astype(jnp.float32)
    for ref in in_refs[1:]:
        total = total + ref[...].astype(jnp.float32)
    total = total.astype(jnp.bfloat16).astype(jnp.float32)
    for step in range(steps):
        out_ref[step] = total[step * rows_dev : (step + 1) * rows_dev].astype(jnp.bfloat16)


def swap(value, mask):
    size = lax.axis_size(PEERS)
    return lax.ppermute(value, PEERS, [(i, i ^ mask) for i in range(size)])


def rows_kernel(begin, whole_ref, part_ref, out_ref):
    size = part_ref.shape[0]
    whole = whole_ref[...].astype(jnp.float32)
    total = whole[begin : begin + size] + part_ref[...].astype(jnp.float32)
    out_ref[...] = total.astype(jnp.bfloat16)


def add_rows(whole, part, begin):
    return pl.pallas_call(
        functools.partial(rows_kernel, begin),
        out_shape=jax.ShapeDtypeStruct(part.shape, jnp.bfloat16),
        in_specs=[VMEM, VMEM],
        out_specs=VMEM,
        compiler_params=pltpu.CompilerParams(vmem_limit_bytes=8 * MIB),
        name="add_rows",
    )(whole, part)


def add(*values):
    total = values[0].astype(jnp.float32)
    for value in values[1:]:
        total = total + value.astype(jnp.float32)
    return total.astype(jnp.bfloat16)


def per_device(
    queries,
    latent_cache,
    new_latents,
    lengths,
    hidden_in,
    first_routes,
    second_routes,
    route_weights,
    gate_weights,
    up_weights,
    down_weights,
    hot_experts,
):
    experts = lax.axis_size("expert")
    devices = lax.axis_size(PEERS)
    steps, rows_dev, width = hidden_in.shape
    rows = steps * rows_dev
    units = down_weights.shape[1]
    bits = devices.bit_length() - 1
    if first_routes.shape[1] != rows_dev:
        begin = lax.axis_index("dp") * rows_dev
        first_routes = lax.dynamic_slice_in_dim(first_routes, begin, rows_dev, 1)
        second_routes = lax.dynamic_slice_in_dim(second_routes, begin, rows_dev, 1)
        route_weights = lax.dynamic_slice_in_dim(route_weights, begin, rows_dev, 1)

    tail = -(-2 * experts // LANES) * LANES
    inputs = (hidden_in, first_routes, second_routes, route_weights)
    packed = pl.pallas_call(
        functools.partial(pack_kernel, experts),
        out_shape=jax.ShapeDtypeStruct((rows, width + tail), jnp.bfloat16),
        in_specs=[HBM] * 5,
        out_specs=VMEM,
        scratch_shapes=[pltpu.VMEM(a.shape, a.dtype) for a in inputs]
        + [pltpu.SMEM(hot_experts.shape, jnp.int32), pltpu.SemaphoreType.DMA((5,))],
        compiler_params=pltpu.CompilerParams(vmem_limit_bytes=4 * MIB),
        name="pack",
    )(*(pltpu.with_memory_space_constraint(a, pltpu.HBM) for a in (*inputs, hot_experts)))

    high = devices // 4
    base = packed
    for bit in range(2, bits - 2):
        base = join([base, swap(base, 1 << bit)])
    size = base.shape[0]
    third = swap(base, 2 * high)
    second = swap(base, 3 * high)
    first = swap(base, 1 * high)
    near = join([base, first])
    far = join([second, third])
    near_y = swap(near, 2)
    far_y = swap(far, 2)
    parts = [near, far, near_y, far_y]
    parts = parts + [swap(part, 1) for part in parts]

    count = 16 * size
    tile = min(256, units)
    half = jax.ShapeDtypeStruct((4 * size, width), jnp.bfloat16)
    keep_far, send_far, keep_near, send_near = pl.pallas_call(
        functools.partial(expert_kernel, experts, tile, len(parts)),
        out_shape=[half] * 4,
        in_specs=[VMEM] * (len(parts) + 3),
        out_specs=[VMEM] * 4,
        scratch_shapes=[
            pltpu.VMEM((count, width + tail), jnp.bfloat16),
            pltpu.VMEM((count, units), jnp.bfloat16),
        ],
        compiler_params=pltpu.CompilerParams(vmem_limit_bytes=24 * MIB),
        cost_estimate=pl.CostEstimate(
            flops=6 * count * width * units,
            bytes_accessed=6 * width * units,
            transcendentals=count * units,
        ),
        name="experts",
    )(*parts, gate_weights, up_weights, down_weights)

    far = add(keep_far, swap(send_far, 1))
    near = add(keep_near, swap(send_near, 1))
    far_third, far_second, far_first = far[3 * size :], far[2 * size : 3 * size], far[: 2 * size]
    third = swap(far_third, 2)
    second = swap(far_second, 2)
    first = swap(far_first, 2)
    third = swap(add_rows(near, third, 3 * size), 2 * high)
    second = swap(add_rows(near, second, 2 * size), 3 * high)
    total = add_rows(near, first, 0)
    pieces = [total[:size], swap(total[size:], 1 * high), second, third]
    for bit in range(bits - 3, 1, -1):
        value = add(*pieces)
        middle = value.shape[0] // 2
        pieces = [value[:middle], swap(value[middle:], 1 << bit)]
    moe_out = pl.pallas_call(
        sum_kernel,
        out_shape=jax.ShapeDtypeStruct((steps, rows_dev, width), jnp.bfloat16),
        in_specs=[VMEM] * len(pieces),
        out_specs=VMEM,
        compiler_params=pltpu.CompilerParams(vmem_limit_bytes=4 * MIB),
        name="total",
    )(*pieces)
    heads = queries.shape[2]
    context = pl.pallas_call(
        attend_kernel,
        out_shape=jax.ShapeDtypeStruct((steps, rows_dev, heads, RANK), jnp.bfloat16),
        in_specs=[VMEM, VMEM, VMEM, SMEM],
        out_specs=HBM,
        scratch_shapes=[
            pltpu.VMEM(
                (rows_dev, latent_cache.shape[2], latent_cache.shape[1]), jnp.bfloat16
            ),
            pltpu.VMEM((steps, rows_dev, heads, RANK), jnp.bfloat16),
            pltpu.SemaphoreType.DMA((rows_dev,)),
        ],
        compiler_params=pltpu.CompilerParams(vmem_limit_bytes=16 * MIB),
        cost_estimate=pl.CostEstimate(
            flops=4 * rows_dev * steps * heads * latent_cache.shape[1] * latent_cache.shape[2],
            bytes_accessed=2 * (2 * queries.size + latent_cache.size),
            transcendentals=rows_dev * steps * heads * latent_cache.shape[1],
        ),
        name="attend",
    )(
        queries,
        jnp.swapaxes(latent_cache, 1, 2),
        new_latents,
        lengths,
    )
    return (context, moe_out)


def solution(mesh):
    every = ("groups", "expert", "dp")
    routed = P(None, ("groups", "expert"), None)
    placed = (
        P(None, every, None, None),
        P(every, None, None),
        P(None, every, None),
        P(every),
        P(None, every, None),
        routed,
        routed,
        routed,
        P("expert", None, "dp"),
        P("expert", None, "dp"),
        P("expert", "dp", None),
        P(),
    )
    return jax.shard_map(
        per_device,
        mesh=mesh,
        in_specs=placed,
        out_specs=(P(None, every, None, None), P(None, every, None)),
        check_vma=False,
    )
```

```python
import functools

import jax
import jax.numpy as jnp
from jax import lax
from jax.experimental import pallas as pl
from jax.experimental.pallas import tpu as pltpu
from jax.sharding import PartitionSpec as P

RANK = 512
SCORE_SCALE = 0.07216878364870322
LANES = 128
SUBLANES = 8
PEERS = ("expert", "dp")
MIB = 1 << 20

VMEM = pl.BlockSpec(memory_space=pltpu.VMEM)
SMEM = pl.BlockSpec(memory_space=pltpu.SMEM)
HBM = pl.BlockSpec(memory_space=pltpu.HBM)
ANY = pl.BlockSpec(memory_space=pl.ANY)


def pack_kernel(experts, *refs):
    sources, out_ref, held, sems = refs[:5], refs[5], refs[6:11], refs[11]
    copies = [
        pltpu.make_async_copy(source, target, sems.at[i])
        for i, (source, target) in enumerate(zip(sources, held))
    ]
    for copy in copies:
        copy.start()
    for copy in copies:
        copy.wait()
    hidden_ref, first_ref, second_ref, weights_ref, hot_ref = held
    steps, rows_dev, width = hidden_ref.shape
    before, _, top = first_ref.shape
    tail = out_ref.shape[1] - width
    column = lax.broadcasted_iota(jnp.int32, (rows_dev, tail), 1)
    rows, marks = [], []
    for step in range(steps):
        if step < before:
            chosen = first_ref[step]
        else:
            chosen = second_ref[step - before]
            for replica in range(hot_ref.shape[0]):
                chosen = jnp.where(chosen == experts + replica, hot_ref[replica], chosen)
        weight = weights_ref[step]
        total = jnp.zeros((rows_dev, tail), jnp.float32)
        for k in range(top):
            picked = chosen[:, k : k + 1]
            here = (column == picked) | (column == picked + experts)
            total = total + jnp.where(here, weight[:, k : k + 1], 0.0)
        high = total.astype(jnp.bfloat16).astype(jnp.float32)
        rows.append(hidden_ref[step].astype(jnp.float32))
        marks.append(jnp.where(column < experts, high, total - high))
    out_ref[:, :width] = jnp.concatenate(rows, axis=0).astype(jnp.bfloat16)
    out_ref[:, width:] = jnp.concatenate(marks, axis=0).astype(jnp.bfloat16)


def attend_kernel(queries_ref, cache_ref, new_ref, lengths_ref, out_hbm, keys, context, sems):
    steps, rows_dev, heads, _ = queries_ref.shape
    slots = cache_ref.shape[2]
    whole = slots - LANES
    fresh = [new_ref[t].astype(jnp.float32) for t in range(steps)]
    spare = jnp.zeros((SUBLANES - steps, keys.shape[1]), jnp.float32)
    target = lax.broadcasted_iota(jnp.int32, (SUBLANES, LANES), 1) - (LANES - steps)
    source = lax.broadcasted_iota(jnp.int32, (SUBLANES, LANES), 0)
    spots = jnp.where(target == source, 1.0, 0.0).astype(jnp.bfloat16)
    spot = lax.broadcasted_iota(jnp.int32, (keys.shape[1], LANES), 1)
    place = lax.broadcasted_iota(jnp.int32, (steps * heads, slots), 1)
    step = lax.broadcasted_iota(jnp.int32, (steps * heads, slots), 0) // heads
    age = place - (slots - steps)
    recent = (age >= 0) & (age <= step)
    copies = []
    for b in range(rows_dev):
        added = jnp.concatenate([f[b : b + 1] for f in fresh] + [spare], axis=0)
        added = lax.dot_general(
            added.astype(jnp.bfloat16),
            spots,
            (((0,), (0,)), ((), ())),
            preferred_element_type=jnp.float32,
        ).astype(jnp.bfloat16)
        keys[b, :, 0:whole] = cache_ref[b, :, 0:whole]
        keys[b, :, whole:] = jnp.where(spot < LANES - steps, cache_ref[b, :, whole:], added)
    scores = []
    for b in range(rows_dev):
        queries = queries_ref[:, b].reshape(steps * heads, queries_ref.shape[3])
        raw = jnp.dot(queries, keys[b], preferred_element_type=jnp.float32)
        scores.append(jnp.where((place < lengths_ref[b]) | recent, raw * SCORE_SCALE, -1e30))
    for b in range(rows_dev):
        weight = jnp.exp(scores[b] - jnp.max(scores[b], axis=1, keepdims=True))
        probs = weight * (1.0 / jnp.sum(weight, axis=1, keepdims=True))
        result = lax.dot_general(
            probs.astype(jnp.bfloat16),
            keys[b, :RANK],
            (((1,), (1,)), ((), ())),
            preferred_element_type=jnp.float32,
        )
        context[:, b] = result.astype(jnp.bfloat16).reshape(steps, heads, RANK)
        copies.append(pltpu.make_async_copy(context.at[:, b], out_hbm.at[:, b], sems.at[b]))
        copies[b].start()
    for copy in copies:
        copy.wait()


def expert_kernel(experts, tile, pieces, *refs):
    x_refs, refs = refs[:pieces], refs[pieces:]
    gate, up, down, keep_far, send_far, keep_near, send_near, x, hidden = refs
    width = down.shape[2]
    units = down.shape[1]
    parts = units // tile
    columns = width // parts
    row = 0
    for x_ref in x_refs:
        x[row : row + x_ref.shape[0]] = x_ref[...]
        row += x_ref.shape[0]
    own = lax.axis_index("expert")
    marks = x[:, width:].astype(jnp.float32)
    column = lax.broadcasted_iota(jnp.int32, marks.shape, 1)
    here = (column == own) | (column == own + experts)
    share = jnp.sum(jnp.where(here, marks, 0.0), axis=1, keepdims=True)
    for j in range(parts):
        cut = slice(j * tile, (j + 1) * tile)
        gate_act = jnp.dot(x[:, :width], gate[0, :, cut], preferred_element_type=jnp.float32)
        up_act = jnp.dot(x[:, :width], up[0, :, cut], preferred_element_type=jnp.float32)
        act = gate_act / (1.0 + jnp.exp(-gate_act)) * up_act
        hidden[:, cut] = act.astype(jnp.bfloat16)
    quarter = keep_far.shape[0]
    for j in range(parts):
        cut = slice(j * columns, (j + 1) * columns)
        out = jnp.dot(hidden[...], down[0, :, cut], preferred_element_type=jnp.float32) * share
        for i, ref in enumerate((keep_near, keep_far, send_near, send_far)):
            ref[:, cut] = out[i * quarter : (i + 1) * quarter].astype(jnp.bfloat16)


def join_kernel(*refs):
    *in_refs, out_ref = refs
    blocks = [ref[...].astype(jnp.float32) for ref in in_refs]
    out_ref[...] = jnp.concatenate(blocks, axis=0).astype(jnp.bfloat16)


def join(blocks):
    size, width = blocks[0].shape
    return pl.pallas_call(
        join_kernel,
        out_shape=jax.ShapeDtypeStruct((len(blocks) * size, width), blocks[0].dtype),
        in_specs=[VMEM] * len(blocks),
        out_specs=VMEM,
        compiler_params=pltpu.CompilerParams(vmem_limit_bytes=8 * MIB),
        cost_estimate=pl.CostEstimate(flops=10000000000, bytes_accessed=0, transcendentals=0),
        name="join",
    )(*blocks)


def sum_kernel(*refs):
    *in_refs, out_ref = refs
    steps, rows_dev, _ = out_ref.shape
    total = in_refs[0][...].astype(jnp.float32)
    for ref in in_refs[1:]:
        total = total + ref[...].astype(jnp.float32)
    total = total.astype(jnp.bfloat16).astype(jnp.float32)
    for step in range(steps):
        out_ref[step] = total[step * rows_dev : (step + 1) * rows_dev].astype(jnp.bfloat16)


def swap(value, mask):
    size = lax.axis_size(PEERS)
    return lax.ppermute(value, PEERS, [(i, i ^ mask) for i in range(size)])


def rows_kernel(begin, whole_ref, part_ref, out_ref):
    size = part_ref.shape[0]
    whole = whole_ref[...].astype(jnp.float32)
    total = whole[begin : begin + size] + part_ref[...].astype(jnp.float32)
    out_ref[...] = total.astype(jnp.bfloat16)


def add_rows(whole, part, begin):
    return pl.pallas_call(
        functools.partial(rows_kernel, begin),
        out_shape=jax.ShapeDtypeStruct(part.shape, jnp.bfloat16),
        in_specs=[VMEM, VMEM],
        out_specs=VMEM,
        compiler_params=pltpu.CompilerParams(vmem_limit_bytes=8 * MIB),
        name="add_rows",
    )(whole, part)


def add(*values):
    total = values[0].astype(jnp.float32)
    for value in values[1:]:
        total = total + value.astype(jnp.float32)
    return total.astype(jnp.bfloat16)


def per_device(
    queries,
    latent_cache,
    new_latents,
    lengths,
    hidden_in,
    first_routes,
    second_routes,
    route_weights,
    gate_weights,
    up_weights,
    down_weights,
    hot_experts,
):
    experts = lax.axis_size("expert")
    devices = lax.axis_size(PEERS)
    steps, rows_dev, width = hidden_in.shape
    rows = steps * rows_dev
    units = down_weights.shape[1]
    bits = devices.bit_length() - 1
    if first_routes.shape[1] != rows_dev:
        begin = lax.axis_index("dp") * rows_dev
        first_routes = lax.dynamic_slice_in_dim(first_routes, begin, rows_dev, 1)
        second_routes = lax.dynamic_slice_in_dim(second_routes, begin, rows_dev, 1)
        route_weights = lax.dynamic_slice_in_dim(route_weights, begin, rows_dev, 1)

    tail = -(-2 * experts // LANES) * LANES
    inputs = (hidden_in, first_routes, second_routes, route_weights)
    packed = pl.pallas_call(
        functools.partial(pack_kernel, experts),
        out_shape=jax.ShapeDtypeStruct((rows, width + tail), jnp.bfloat16),
        in_specs=[HBM] * 5,
        out_specs=VMEM,
        scratch_shapes=[pltpu.VMEM(a.shape, a.dtype) for a in inputs]
        + [pltpu.SMEM(hot_experts.shape, jnp.int32), pltpu.SemaphoreType.DMA((5,))],
        compiler_params=pltpu.CompilerParams(vmem_limit_bytes=4 * MIB),
        name="pack",
    )(*(pltpu.with_memory_space_constraint(a, pltpu.HBM) for a in (*inputs, hot_experts)))

    high = devices // 4
    base = packed
    for bit in range(2, bits - 2):
        base = join([base, swap(base, 1 << bit)])
    size = base.shape[0]
    third = swap(base, 2 * high)
    second = swap(base, 3 * high)
    first = swap(base, 1 * high)
    near = join([base, first])
    far = join([second, third])
    near_y = swap(near, 2)
    far_y = swap(far, 2)
    parts = [near, far, near_y, far_y]
    parts = parts + [swap(part, 1) for part in parts]

    count = 16 * size
    tile = min(512, units)
    half = jax.ShapeDtypeStruct((4 * size, width), jnp.bfloat16)
    keep_far, send_far, keep_near, send_near = pl.pallas_call(
        functools.partial(expert_kernel, experts, tile, len(parts)),
        out_shape=[half] * 4,
        in_specs=[VMEM] * (len(parts) + 3),
        out_specs=[VMEM] * 4,
        scratch_shapes=[
            pltpu.VMEM((count, width + tail), jnp.bfloat16),
            pltpu.VMEM((count, units), jnp.bfloat16),
        ],
        compiler_params=pltpu.CompilerParams(vmem_limit_bytes=24 * MIB),
        cost_estimate=pl.CostEstimate(
            flops=6 * count * width * units,
            bytes_accessed=6 * width * units,
            transcendentals=count * units,
        ),
        name="experts",
    )(*parts, gate_weights, up_weights, down_weights)

    far = add(keep_far, swap(send_far, 1))
    near = add(keep_near, swap(send_near, 1))
    far_third, far_second, far_first = far[3 * size :], far[2 * size : 3 * size], far[: 2 * size]
    third = swap(far_third, 2)
    second = swap(far_second, 2)
    first = swap(far_first, 2)
    third = swap(add_rows(near, third, 3 * size), 2 * high)
    second = swap(add_rows(near, second, 2 * size), 3 * high)
    total = add_rows(near, first, 0)
    pieces = [total[:size], swap(total[size:], 1 * high), second, third]
    for bit in range(bits - 3, 1, -1):
        value = add(*pieces)
        middle = value.shape[0] // 2
        pieces = [value[:middle], swap(value[middle:], 1 << bit)]
    moe_out = pl.pallas_call(
        sum_kernel,
        out_shape=jax.ShapeDtypeStruct((steps, rows_dev, width), jnp.bfloat16),
        in_specs=[VMEM] * len(pieces),
        out_specs=VMEM,
        compiler_params=pltpu.CompilerParams(vmem_limit_bytes=4 * MIB),
        name="total",
    )(*pieces)
    heads = queries.shape[2]
    context = pl.pallas_call(
        attend_kernel,
        out_shape=jax.ShapeDtypeStruct((steps, rows_dev, heads, RANK), jnp.bfloat16),
        in_specs=[VMEM, VMEM, VMEM, SMEM],
        out_specs=HBM,
        scratch_shapes=[
            pltpu.VMEM(
                (rows_dev, latent_cache.shape[2], latent_cache.shape[1]), jnp.bfloat16
            ),
            pltpu.VMEM((steps, rows_dev, heads, RANK), jnp.bfloat16),
            pltpu.SemaphoreType.DMA((rows_dev,)),
        ],
        compiler_params=pltpu.CompilerParams(vmem_limit_bytes=16 * MIB),
        cost_estimate=pl.CostEstimate(
            flops=4 * rows_dev * steps * heads * latent_cache.shape[1] * latent_cache.shape[2],
            bytes_accessed=2 * (2 * queries.size + latent_cache.size),
            transcendentals=rows_dev * steps * heads * latent_cache.shape[1],
        ),
        name="attend",
    )(
        queries,
        jnp.swapaxes(latent_cache, 1, 2),
        new_latents,
        lengths,
    )
    return (context, moe_out)


def solution(mesh):
    every = ("groups", "expert", "dp")
    routed = P(None, ("groups", "expert"), None)
    placed = (
        P(None, every, None, None),
        P(every, None, None),
        P(None, every, None),
        P(every),
        P(None, every, None),
        routed,
        routed,
        routed,
        P("expert", None, "dp"),
        P("expert", None, "dp"),
        P("expert", "dp", None),
        P(),
    )
    return jax.shard_map(
        per_device,
        mesh=mesh,
        in_specs=placed,
        out_specs=(P(None, every, None, None), P(None, every, None)),
        check_vma=False,
    )
```
